32 devices in a mesh: groups: 2 (over x), expert: 16 (over z, y, core).
Axes of the slice: x: 2, y: 2, z: 4, core: 2. Of those that a mesh axis runs over, the one named last changes fastest.
Arguments:
- acts: bfloat16 [4096, 2048], P(('groups', 'expert')), parts along dimension 0, may hold values from -6 to 6
- out_grad: bfloat16 [4096, 2048], P(('groups', 'expert')), parts along dimension 0, may hold values from -6 to 6
- routes: int32 [4096, 8], P(('groups', 'expert')), parts along dimension 0, may hold values from 0 to 15, all different within a row; in each aligned block of 128 rows (0 to 127, 128 to 255, ...) at most 128 rows name the same one
- route_weight: float32 [4096, 8], P(('groups', 'expert')), parts along dimension 0, may hold values from 0.05 to 1
- w_gate: bfloat16 [16, 2048, 768], P('expert'), may hold values from -0.125 to 0.125
- w_up: bfloat16 [16, 2048, 768], P('expert'), may hold values from -0.125 to 0.125
- proj_in: bfloat16 [16, 768, 32], P('expert'), may hold values from -4 to 4
- proj_out: bfloat16 [2048, 32], replicated, may hold values from -0.125 to 0.125
Outputs:
- sketches: float32 [16, 4, 1024], P('expert', 'groups'), parts along dimension 1
The draws below stay inside these ranges and needn't reach their ends.
There are 2 independent parts, one for each index of `groups`. The reference program is written for one: setup_inputs(seed, part) draws one part's arguments, and reference() takes and returns one part's arrays. A program takes and returns all parts, laid end to end along the dimension named above; an argument that names none is the same for every part. Nothing has to cross between parts.
Inputs may be any that keep to these rules, and one draw needn't show every extreme that they name: `routes`: in the 128 tokens of one device (an aligned block) no expert is named by more than 128 tokens, a bound that some block reaches; a token names 8 different experts.
All inputs are finite; a program needn't handle non-finite values.
Results may differ from the reference program's by a relative error of at most 0.005.
Values may be sent and summed in bfloat16 or wider, within the bound.
A program may use at most 128 MiB of HBM per device.

```python
import math
import jax
import jax.numpy as jnp
import numpy as np
from jax import lax

D = 2048
FF = 768
TOP = 8
RANK = 32
EXAMPLES = 2
TOK_DEV = 128
EXPERTS = 16
CAP = 128
TOKENS = 2048
LENGTH = 1024
N_EXPERT = 16


def draw_proj_in(key, part):
    key = jax.random.fold_in(key, 7)
    noise = jax.random.normal(key, (EXPERTS, FF, RANK), jnp.float32)
    ramp = jnp.arange(EXPERTS, dtype=jnp.float32) / max(EXPERTS - 1, 1)
    lift = jnp.sqrt(1.0 + 2.0 * ramp)
    return (noise * lift[:, None, None] * FF ** (-0.5)).astype(jnp.bfloat16)


def block_levels(rng, dims, pieces, low, high):
    level, own = 1.0, jax.random.fold_in(rng, 6)
    for axis_at, shards_of in pieces:
        draws = jnp.exp(jax.random.uniform(jax.random.fold_in(own, axis_at), (shards_of,), jnp.float32, low / len(pieces), high / len(pieces)))
        level = level * jnp.repeat(draws, dims[axis_at] // shards_of).reshape([-1 if axis == axis_at else 1 for axis in range(len(dims))])
    return level


def deal_out(key, own, number, rows, amount, top, bound, slope):
    sequence = jax.random.permutation(key, amount)
    crowded, usual = portions_of(amount, rows * top, bound, slope, True), portions_of(amount, rows * top, bound, slope, False)
    places = jnp.arange(amount)

    def named(tallies, rotation):
        used = int((tallies > 0).sum())
        fixed = max(1, used // 4)
        moved = fixed + (places - fixed + rotation * (used - fixed)) % max(1, amount - fixed)
        return jnp.zeros((amount,), jnp.int32).at[sequence[jnp.where(places < fixed, places, moved)]].set(jnp.asarray(tallies, jnp.int32))

    tallies = jnp.where(number % 4 == 0, named(crowded, number // 4), named(usual, number - number // 4 - 1))
    mixed = jax.random.permutation(jax.random.fold_in(own, 3), amount)
    donor, receiver = mixed[0:amount // 2 * 2:2], mixed[1:amount // 2 * 2:2]
    slack = jnp.minimum(tallies[donor] - 1, bound - tallies[receiver]) // 2
    slack = jnp.where((donor == sequence[0]) | (receiver == sequence[0]) | (tallies[receiver] == 0), 0, jnp.maximum(slack, 0))
    moved = jax.random.randint(jax.random.fold_in(own, 4), (amount // 2,), 0, 1 << 20) % (slack + 1)
    tallies = tallies.at[donor].add(-moved).at[receiver].add(moved)
    labels = jnp.searchsorted(jnp.cumsum(tallies), jnp.arange(rows * top), side="right").astype(jnp.int32)
    grid = labels.reshape(top, rows).T
    grid = grid[jax.random.permutation(jax.random.fold_in(own, 1), rows)]
    rotation = jax.random.randint(jax.random.fold_in(own, 2), (rows, 1), 0, top)
    return jnp.take_along_axis(grid, (jnp.arange(top)[None, :] + rotation) % top, axis=1)


def portions_of(number_of, total, most, lean, full):
    loads = [(1 << 20) // math.isqrt(grade ** lean) + 1 for grade in range(1, number_of + 1)]
    largest = most if full else min(most, max(-(-total // number_of), total * loads[0] // sum(loads)))
    least = 1 if total - largest >= number_of - 1 else 0
    holding, spare = [largest] + [least] * (number_of - 1), total - largest - least * (number_of - 1)
    while spare > 0:
        movable = [i for i in range(1, number_of) if holding[i] < largest] or [i for i in range(1, number_of) if holding[i] < most]
        mass, budget = sum([loads[i] for i in movable]), spare
        for i in movable:
            extra = min(most - holding[i], max(1, budget * loads[i] // mass), spare)
            holding[i] = holding[i] + extra
            spare = spare - extra
    return np.array(holding)


def centred(rng, extent, deviation, limit, cuts=(), kind=jnp.bfloat16):
    factor_of = block_levels(rng, extent, cuts, -0.22, 0.18) if cuts else 1.0
    array = jax.random.normal(rng, extent, jnp.float32) * deviation * factor_of
    return jnp.minimum(jnp.maximum(array, -limit), limit).astype(kind)


def setup_inputs(seed: int = 0, part: int = 0) -> dict:
    splits = jax.random.split(jax.random.key(seed), 9)
    part_keys = jax.random.split(jax.random.fold_in(splits[8], part), 9)
    acts = centred(part_keys[0], (TOKENS, D), 1.0, 6.0, ((0, 16),))
    out_grad = centred(part_keys[1], (TOKENS, D), 1.0, 6.0, ((0, 16),))
    routes_keys = jax.random.split(jax.random.fold_in(part_keys[2], 1), TOKENS // TOK_DEV)
    routes_turns = jax.random.permutation(jax.random.fold_in(part_keys[2], 3), TOKENS // TOK_DEV)
    routes = jax.vmap(lambda own, number: deal_out(jax.random.fold_in(part_keys[2], 2), own, number, TOK_DEV, EXPERTS, TOP, CAP, 2))(routes_keys, routes_turns).reshape((TOKENS, TOP))
    route_weight = jnp.clip(0.05 + 0.95 * jax.random.uniform(part_keys[3], (TOKENS, TOP), jnp.float32) ** block_levels(part_keys[3], (TOKENS, TOP), ((0, 16),), -0.2, 0.2), 0.05, 1.0)
    w_gate = centred(splits[4], (EXPERTS, D, FF), D ** -0.5, 0.125, ((0, 16),))
    w_up = centred(splits[5], (EXPERTS, D, FF), D ** -0.5, 0.125, ((0, 16),))
    proj_in = draw_proj_in(jax.random.fold_in(splits[8], 71), part)
    proj_out = centred(splits[7], (D, RANK), D ** -0.5, 0.125)
    return dict(acts=acts, out_grad=out_grad, routes=routes, route_weight=route_weight, w_gate=w_gate, w_up=w_up, proj_in=proj_in, proj_out=proj_out)


def reference(acts, out_grad, routes, route_weight, w_gate, w_up, proj_in, proj_out):
    flat = routes.reshape(-1)
    weights_flat = route_weight.reshape(-1)
    rows_max = N_EXPERT * CAP

    def one_expert(expert):
        hit = flat == expert
        picked = jnp.nonzero(hit, size=rows_max, fill_value=0)[0].astype(jnp.int32)
        live = jnp.arange(rows_max, dtype=jnp.int32) < jnp.sum(hit.astype(jnp.int32))
        token_of = picked // TOP
        rows = acts[token_of]
        gate = jnp.dot(rows, w_gate[expert], preferred_element_type=jnp.float32)
        upper = jnp.dot(rows, w_up[expert], preferred_element_type=jnp.float32)
        hidden = (jax.nn.silu(gate) * upper).astype(jnp.bfloat16)
        reduced = jnp.dot(hidden, proj_in[expert], preferred_element_type=jnp.float32)
        reduced = jnp.where(live[:, None], reduced, jnp.float32(0.0))
        scaled = (weights_flat[picked][:, None] * out_grad[token_of].astype(jnp.float32)).astype(jnp.bfloat16)
        projected = jnp.dot(scaled, proj_out, preferred_element_type=jnp.float32).astype(jnp.bfloat16)
        example = token_of // LENGTH
        member = ((example[:, None] == jnp.arange(EXAMPLES, dtype=jnp.int32)[None, :]) & live[:, None]).astype(jnp.float32)
        spread = (member[:, :, None] * reduced[:, None, :]).reshape(rows_max, EXAMPLES * RANK)
        sketch = jnp.dot(spread.T, projected.astype(jnp.float32), precision=lax.Precision.HIGHEST)
        return sketch.reshape(EXAMPLES, RANK * RANK)
    raw = lax.map(one_expert, jnp.arange(EXPERTS, dtype=jnp.int32))
    power = lax.optimization_barrier(jnp.sum(raw * raw, axis=(0, 2)))
    factor = lax.rsqrt(power / (EXPERTS * RANK * RANK) + 1e-06)
    return raw * factor[None, :, None]
```

```python
import functools

import jax
import jax.numpy as jnp
from jax import lax
from jax.experimental import pallas as pl
from jax.experimental.pallas import tpu as pltpu
from jax.sharding import PartitionSpec as P

EXAMPLES = 2
MESH = pl.DeviceIdType.MESH
RIGHT, LEFT, ACROSS, SIBLING = 0, 1, 2, 3


def row_chunks(rows, lines):
    half = rows // 2
    if lines == 1:
        return ((0, half), (half, rows - half)), 2
    late = rows // 8
    return ((0, half), (half, rows - half - late), (rows - late, late)), 2


def kernel(
    devices, lines, acts_ref, grad_ref, routes_ref, weight_ref, gate_ref, up_ref, in_ref, out_ref,
    result_ref,
    acts, grad, routes, weight, gate, up, proj_in, proj_out,
    sides_out, sides, total, powers,
    local_sem, arrive_sem, send_sem, side_arrive, side_send, power_arrive, power_send,
):
    length = devices // 2 // lines
    chips = devices // 2
    rows = acts.shape[1]
    side = sides.shape[1]
    width = gate.shape[1]
    top = routes.shape[1]
    chunks, first_count = row_chunks(rows, lines)
    me = lax.axis_index("expert")
    core = lax.rem(me, 2)
    chip = me // 2
    line = lax.rem(chip, lines)
    place = chip // lines

    def block(at_place, at_line, at_core):
        return (jnp.clip(at_place, 0, length - 1) * lines + at_line) * 2 + at_core

    def sibling_of(index):
        return index + 1 - 2 * lax.rem(index, 2)

    loads = [
        pltpu.make_async_copy(grad_ref, grad, local_sem.at[0]),
        pltpu.make_async_copy(out_ref, proj_out, local_sem.at[1]),
        pltpu.make_async_copy(routes_ref, routes, local_sem.at[2]),
        pltpu.make_async_copy(weight_ref, weight, local_sem.at[3]),
        pltpu.make_async_copy(acts_ref, acts.at[me], local_sem.at[4]),
        pltpu.make_async_copy(gate_ref.at[0], gate, local_sem.at[5]),
        pltpu.make_async_copy(up_ref.at[0], up, local_sem.at[6]),
        pltpu.make_async_copy(in_ref.at[0], proj_in, local_sem.at[7]),
    ]
    for load in loads:
        load.start()

    barrier = pltpu.get_barrier_semaphore()

    @pl.loop(1, devices)
    def _(i):
        other = lax.rem(me + i, devices)
        pl.semaphore_signal(barrier, inc=1, device_id={"expert": other}, device_id_type=MESH)

    pl.semaphore_wait(barrier, devices - 1)

    targets = (
        block(place + 1, line, core),
        block(place - 1, line, core),
        block(place, lines - 1 - line, core),
        sibling_of(me),
    )
    has_right = place < length - 1
    has_left = place > 0
    other_line = lines - 1 - line

    def transfer(index, chunk, way, own=False):
        start, count = chunks[chunk]
        rows_of = pl.ds(start, count)
        source = acts_ref.at[rows_of] if own else acts.at[index, rows_of]
        return pltpu.make_async_remote_copy(
            src_ref=source,
            dst_ref=acts.at[index, rows_of],
            send_sem=send_sem.at[way, index, chunk],
            recv_sem=arrive_sem.at[index, chunk],
            device_id={"expert": targets[way]},
            device_id_type=MESH,
        )

    def own_moves():
        moves = []
        for chunk in range(first_count, len(chunks)):
            moves.append((True, me, chunk, ACROSS))
        for chunk in range(len(chunks)):
            moves.append((has_right, me, chunk, RIGHT))
            moves.append((has_left, me, chunk, LEFT))
            if chunk < first_count and lines > 1:
                moves.append((True, me, chunk, ACROSS))
            moves.append((True, me, chunk, SIBLING))
        return moves

    def arrivals(distance):
        listed = []
        for chunk in range(first_count, len(chunks)):
            present = distance == 1
            index = block(place, other_line, core)
            moves = [
                (present & has_right, index, chunk, RIGHT),
                (present & has_left, index, chunk, LEFT),
                (present, index, chunk, SIBLING),
            ]
            listed.append((present, index, chunk, moves))
        for chunk in range(len(chunks)):
            late = chunk >= first_count
            for way in (RIGHT, LEFT):
                at = place - distance if way == RIGHT else place + distance
                inside = (at >= 0) if way == RIGHT else (at < length)
                onward = has_right if way == RIGHT else has_left
                present = (distance >= 1) & inside & (distance < length)
                index = block(at, line, core)
                moves = [(present & onward, index, chunk, way)]
                if lines > 1 and not late:
                    moves.append((present, index, chunk, ACROSS))
                moves.append((present, index, chunk, SIBLING))
                listed.append((present, index, chunk, moves))
                if lines == 1:
                    continue
                if late:
                    index = block(at, other_line, core)
                    moves = [(present & onward, index, chunk, way), (present, index, chunk, SIBLING)]
                    listed.append((present, index, chunk, moves))
                back = distance - 1
                at = place - back if way == RIGHT else place + back
                inside = (at >= 0) if way == RIGHT else (at < length)
                index = block(at, other_line, core)
                if not late:
                    present = (distance >= 1) & inside
                    if way == LEFT:
                        present = present & (back >= 1)
                    listed.append((present, index, chunk, [(present, index, chunk, SIBLING)]))
        return listed

    for present, index, chunk, way in own_moves():
        @pl.when(present)
        def _(index=index, chunk=chunk, way=way):
            transfer(index, chunk, way, own=True).start()

    for load in loads[:4]:
        load.wait()
    projected = jnp.dot(grad[...], proj_out[...], preferred_element_type=jnp.float32).T
    names = routes[...].astype(jnp.float32).T
    scales = weight[...].T

    @pl.loop(0, devices)
    def _(expert):
        hit = names == lax.convert_element_type(expert, jnp.float32)
        scale = jnp.sum(jnp.where(hit, scales, 0.0), axis=0, keepdims=True)
        sides_out[expert] = (projected * scale).astype(jnp.bfloat16)

    def side_move(other):
        return pltpu.make_async_remote_copy(
            src_ref=sides_out.at[other],
            dst_ref=sides.at[me],
            send_sem=side_send.at[other],
            recv_sem=side_arrive.at[me],
            device_id={"expert": other},
            device_id_type=MESH,
        )

    @pl.loop(1, devices)
    def _(i):
        side_move(lax.rem(me + i, devices)).start()

    sides[me] = sides_out[me]
    total[...] = jnp.zeros_like(total)
    for load in loads[4:]:
        load.wait()

    def compute(chip_index):
        x = acts[pl.ds(2 * chip_index, 2)].reshape(2 * rows, acts.shape[2])
        pair = sides[pl.ds(2 * chip_index, 2)]
        pair = jnp.concatenate([pair[0], pair[1]], axis=1)
        example = chip_index // (chips // EXAMPLES)
        step = 256
        for start in range(0, width, step):
            gated = jnp.dot(x, gate[:, start : start + step], preferred_element_type=jnp.float32)
            upper = jnp.dot(x, up[:, start : start + step], preferred_element_type=jnp.float32)
            hidden = (gated / (1.0 + jnp.exp(-gated)) * upper).astype(jnp.bfloat16)
            total[example, :, start : start + step] += jnp.dot(
                pair, hidden, preferred_element_type=jnp.float32
            )

    @pl.loop(0, length + (1 if lines > 1 else 0))
    def _(distance):
        for present, index, chunk, moves in arrivals(distance):
            @pl.when(present)
            def _(index=index, chunk=chunk):
                transfer(index, chunk, SIBLING).wait_recv()

            for wanted, index, chunk, way in moves:
                @pl.when(wanted)
                def _(index=index, chunk=chunk, way=way):
                    transfer(index, chunk, way).start()

        @pl.loop(0, 4 if lines > 1 else 2)
        def _(unit):
            partner = unit // 2
            leftward = lax.rem(unit, 2)
            far = distance - partner
            at = place - far + 2 * far * leftward
            present = (far >= leftward) & (at >= 0) & (at < length)
            index = block(at, line + partner * (other_line - line), core)

            @pl.when(present)
            def _():
                for chunk in range(len(chunks)):
                    transfer(sibling_of(index), chunk, SIBLING).wait_recv()

                pltpu.make_async_copy(
                    sides.at[sibling_of(index)],
                    sides.at[sibling_of(index)],
                    side_arrive.at[sibling_of(index)],
                ).wait()

                @pl.when(index != me)
                def _():
                    pltpu.make_async_copy(
                        sides.at[index], sides.at[index], side_arrive.at[index]
                    ).wait()

                compute(index // 2)

    raw = []
    matrix = proj_in[...].astype(jnp.float32)
    for example in range(EXAMPLES):
        turned = jnp.dot(
            total[example],
            matrix,
            preferred_element_type=jnp.float32,
            precision=lax.Precision.HIGHEST,
        )
        raw.append(turned.T)
    own_power = [jnp.sum(one * one, keepdims=True) for one in raw]
    row_of = lax.broadcasted_iota(jnp.int32, (8, 128), 0)
    tile = jnp.zeros((8, 128), jnp.float32)
    for example in range(EXAMPLES):
        tile = jnp.where(row_of == example, own_power[example], tile)
    powers[me] = tile

    def power_move(other):
        return pltpu.make_async_remote_copy(
            src_ref=powers.at[me],
            dst_ref=powers.at[me],
            send_sem=power_send.at[other],
            recv_sem=power_arrive.at[me],
            device_id={"expert": other},
            device_id_type=MESH,
        )

    @pl.loop(1, devices)
    def _(i):
        power_move(lax.rem(me + i, devices)).start()

    for present, index, chunk, way in own_moves():
        @pl.when(present)
        def _(index=index, chunk=chunk, way=way):
            transfer(index, chunk, way, own=True).wait_send()

    @pl.loop(0, length + (1 if lines > 1 else 0))
    def _(distance):
        for _, _, _, moves in arrivals(distance):
            for wanted, index, chunk, way in moves:
                @pl.when(wanted)
                def _(index=index, chunk=chunk, way=way):
                    transfer(index, chunk, way).wait_send()

    @pl.loop(1, devices)
    def _(i):
        other = lax.rem(me + i, devices)
        side_move(other).wait_send()
        power_move(other).wait_send()
        pltpu.make_async_copy(powers.at[other], powers.at[other], power_arrive.at[other]).wait()

    power = jnp.sum(powers[...], axis=0)
    factor = lax.rsqrt(power / (devices * side * side) + 1e-06)
    for example in range(EXAMPLES):
        result_ref[example] = raw[example] * factor[example : example + 1, :1]


def on_device(devices, lines, acts, out_grad, routes, route_weight, w_gate, w_up, proj_in, proj_out):
    rows, depth = acts.shape
    top = routes.shape[1]
    width = w_gate.shape[2]
    side = proj_out.shape[1]
    pieces = len(row_chunks(rows, lines)[0])
    dma = pltpu.SemaphoreType.DMA
    scaled = pl.pallas_call(
        functools.partial(kernel, devices, lines),
        out_shape=jax.ShapeDtypeStruct((EXAMPLES, side, side), jnp.float32),
        in_specs=[pl.BlockSpec(memory_space=pl.ANY)] * 8,
        out_specs=pl.BlockSpec(memory_space=pltpu.VMEM),
        scratch_shapes=[
            pltpu.VMEM((devices, rows, depth), jnp.bfloat16),
            pltpu.VMEM((rows, depth), jnp.bfloat16),
            pltpu.VMEM((rows, top), jnp.int32),
            pltpu.VMEM((rows, top), jnp.float32),
            pltpu.VMEM((depth, width), jnp.bfloat16),
            pltpu.VMEM((depth, width), jnp.bfloat16),
            pltpu.VMEM((width, side), jnp.bfloat16),
            pltpu.VMEM((depth, side), jnp.bfloat16),
            pltpu.VMEM((devices, side, rows), jnp.bfloat16),
            pltpu.VMEM((devices, side, rows), jnp.bfloat16),
            pltpu.VMEM((EXAMPLES, side, width), jnp.float32),
            pltpu.VMEM((devices, 8, 128), jnp.float32),
            dma((8,)),
            dma((devices, pieces)),
            dma((4, devices, pieces)),
            dma((devices,)),
            dma((devices,)),
            dma((devices,)),
            dma((devices,)),
        ],
        compiler_params=pltpu.CompilerParams(
            collective_id=0, has_side_effects=True, vmem_limit_bytes=60 * 1024 * 1024
        ),
        cost_estimate=pl.CostEstimate(
            flops=2 * devices * rows * depth * 2 * width,
            bytes_accessed=2 * depth * width * 2,
            transcendentals=devices * rows * width,
        ),
    )(acts, out_grad, routes, route_weight, w_gate, w_up, proj_in, proj_out)
    return scaled.reshape(1, EXAMPLES, side * side)


def solution(mesh):
    devices = mesh.shape["expert"]
    lines = 2 if devices == 16 else 1
    return jax.shard_map(
        functools.partial(on_device, devices, lines),
        mesh=mesh,
        in_specs=(
            P(("groups", "expert"), None),
            P(("groups", "expert"), None),
            P(("groups", "expert"), None),
            P(("groups", "expert"), None),
            P("expert", None, None),
            P("expert", None, None),
            P("expert", None, None),
            P(),
        ),
        out_specs=P("expert", "groups", None),
        check_vma=False,
    )
```

```python
import functools

import jax
import jax.numpy as jnp
from jax import lax
from jax.experimental import pallas as pl
from jax.experimental.pallas import tpu as pltpu
from jax.sharding import PartitionSpec as P

EXAMPLES = 2
MESH = pl.DeviceIdType.MESH
RIGHT, LEFT, ACROSS, SIBLING = 0, 1, 2, 3


def row_chunks(rows, lines):
    part = rows // 4
    if lines == 1:
        return tuple((part * i, part) for i in range(4)), 4
    late = rows // 8
    first = rows - late - 2 * part
    return ((0, first), (first, part), (first + part, part), (rows - late, late)), 3


def kernel(
    devices, lines, acts_ref, grad_ref, routes_ref, weight_ref, gate_ref, up_ref, in_ref, out_ref,
    result_ref,
    acts, grad, routes, weight, gate, up, proj_in, proj_out,
    notes, total, powers,
    local_sem, arrive_sem, send_sem, power_arrive, power_send,
):
    length = devices // 2 // lines
    chips = devices // 2
    rows = acts.shape[1]
    side = proj_out.shape[0]
    width = gate.shape[1]
    chunks, first_count = row_chunks(rows, lines)
    me = lax.axis_index("expert")
    core = lax.rem(me, 2)
    chip = me // 2
    line = lax.rem(chip, lines)
    place = chip // lines

    def block(at_place, at_line, at_core):
        return (jnp.clip(at_place, 0, length - 1) * lines + at_line) * 2 + at_core

    def sibling_of(index):
        return index + 1 - 2 * lax.rem(index, 2)

    loads = [
        pltpu.make_async_copy(acts_ref, acts.at[me], local_sem.at[4]),
        pltpu.make_async_copy(grad_ref, grad, local_sem.at[0]),
        pltpu.make_async_copy(out_ref, proj_out, local_sem.at[1]),
        pltpu.make_async_copy(routes_ref, routes, local_sem.at[2]),
        pltpu.make_async_copy(weight_ref, weight, local_sem.at[3]),
        pltpu.make_async_copy(gate_ref.at[0], gate, local_sem.at[5]),
        pltpu.make_async_copy(up_ref.at[0], up, local_sem.at[6]),
        pltpu.make_async_copy(in_ref.at[0], proj_in, local_sem.at[7]),
    ]
    for load in loads:
        load.start()

    targets = (
        block(place + 1, line, core),
        block(place - 1, line, core),
        block(place, lines - 1 - line, core),
        sibling_of(me),
    )
    has_right = place < length - 1
    has_left = place > 0
    other_line = lines - 1 - line

    neighbours = [(has_right, RIGHT), (has_left, LEFT), (True, SIBLING)]
    if lines > 1:
        neighbours.append((True, ACROSS))
    barrier = pltpu.get_barrier_semaphore()
    for present, way in neighbours:
        @pl.when(present)
        def _(way=way):
            pl.semaphore_signal(
                barrier, inc=1, device_id={"expert": targets[way]}, device_id_type=MESH
            )

    loads[0].wait()
    others = 1 + (lines - 1) + has_right.astype(jnp.int32) + has_left.astype(jnp.int32)
    pl.semaphore_wait(barrier, others)

    notes_chunk = len(chunks)

    def transfer(index, chunk, way):
        if chunk == notes_chunk:
            moved = notes.at[index]
        else:
            start, count = chunks[chunk]
            moved = acts.at[index, pl.ds(start, count)]
        return pltpu.make_async_remote_copy(
            src_ref=moved,
            dst_ref=moved,
            send_sem=send_sem.at[way, index, chunk],
            recv_sem=arrive_sem.at[index, chunk],
            device_id={"expert": targets[way]},
            device_id_type=MESH,
        )

    def arrivals(distance, step):
        listed = []
        own = distance == 0
        for chunk in (step,) if step < notes_chunk - 1 else (step, notes_chunk):
            late = first_count <= chunk < notes_chunk
            if chunk == 0:
                for after in range(first_count, len(chunks)):
                    listed.append((False, me, after, [(own, me, after, ACROSS)]))
            for way in (RIGHT, LEFT):
                at = place - distance if way == RIGHT else place + distance
                onward = has_right if way == RIGHT else has_left
                inside = (distance >= 0) & ((at >= 0) if way == RIGHT else (at < length))
                inside = inside & (distance < length)
                once = inside if way == RIGHT else inside & (distance >= 1)
                index = block(at, line, core)
                moves = [(inside & onward, index, chunk, way)]
                if lines > 1 and not late:
                    moves.append((once, index, chunk, ACROSS))
                moves.append((once, index, chunk, SIBLING))
                listed.append((inside & (distance >= 1), index, chunk, moves))
            if lines == 1:
                continue
            for way in (RIGHT, LEFT):
                onward = has_right if way == RIGHT else has_left
                if late:
                    at = place - distance if way == RIGHT else place + distance
                    inside = (distance >= 0) & ((at >= 0) if way == RIGHT else (at < length))
                    inside = inside & (distance < length)
                    once = inside if way == RIGHT else inside & (distance >= 1)
                    index = block(at, other_line, core)
                    moves = [(inside & onward, index, chunk, way), (once, index, chunk, SIBLING)]
                    listed.append((once, index, chunk, moves))
                else:
                    back = distance - 1
                    at = place - back if way == RIGHT else place + back
                    inside = (at >= 0) if way == RIGHT else (at < length)
                    inside = inside & (back >= (0 if way == RIGHT else 1)) & (back < length)
                    index = block(at, other_line, core)
                    listed.append((inside, index, chunk, [(inside, index, chunk, SIBLING)]))
        return listed

    def project():
        for load in loads[1:5]:
            load.wait()
        projected = lax.dot_general(
            proj_out[...], grad[...], (((1,), (1,)), ((), ())), preferred_element_type=jnp.float32
        )
        names = routes[...]
        scales = weight[...]
        notes[me, :side] = projected
        for expert in range(devices):
            hit = names == expert
            notes[me, side + expert : side + expert + 1] = jnp.sum(
                jnp.where(hit, scales, 0.0), axis=0, keepdims=True
            )
        total[...] = jnp.zeros_like(total)
        for load in loads[5:]:
            load.wait()

    def compute(chip_index):
        x = acts[pl.ds(2 * chip_index, 2)].reshape(2 * rows, acts.shape[2])
        pair = [
            notes[2 * chip_index + part, :side] * notes[2 * chip_index + part, pl.ds(side + me, 1)]
            for part in range(2)
        ]
        pair = jnp.concatenate(pair, axis=1).astype(jnp.bfloat16)
        example = chip_index // (chips // EXAMPLES)
        step = 256
        for start in range(0, width, step):
            gated = jnp.dot(x, gate[:, start : start + step], preferred_element_type=jnp.float32)
            upper = jnp.dot(x, up[:, start : start + step], preferred_element_type=jnp.float32)
            hidden = (gated / (1.0 + jnp.exp(-gated)) * upper).astype(jnp.bfloat16)
            total[example, :, start : start + step] += jnp.dot(
                pair, hidden, preferred_element_type=jnp.float32
            )

    def wait_sent(distance, step, ways):
        for _, _, _, moves in arrivals(distance, step):
            for wanted, index, chunk, way in moves:
                if way in ways:
                    @pl.when(wanted)
                    def _(index=index, chunk=chunk, way=way):
                        transfer(index, chunk, way).wait_send()

    steps = len(chunks)
    last = length + (1 if lines > 1 else 0)

    @pl.loop(0, last + 1)
    def _(distance):
        for step in range(steps):
            if step == 2:
                pl.when(distance == 0)(project)
            before = distance if step >= 2 else distance - 1
            wait_sent(before, (step - 2) % steps, (RIGHT, LEFT, ACROSS))
            for present, index, chunk, moves in arrivals(distance, step):
                if present is not False:
                    @pl.when(present)
                    def _(index=index, chunk=chunk):
                        transfer(index, chunk, SIBLING).wait_recv()

                for wanted, index, chunk, way in moves:
                    @pl.when(wanted)
                    def _(index=index, chunk=chunk, way=way):
                        transfer(index, chunk, way).start()

            if step >= (4 if lines > 1 else 2):
                continue
            partner = step // 2
            far = distance - 1 - partner
            at = place + far if step % 2 else place - far
            present = (far >= step % 2) & (at >= 0) & (at < length)
            index = block(at, other_line if partner else line, core)

            @pl.when(present)
            def _(index=index):
                for chunk in range(len(chunks) + 1):
                    transfer(sibling_of(index), chunk, SIBLING).wait_recv()

                compute(index // 2)

    raw = []
    matrix = proj_in[...].astype(jnp.float32)
    for example in range(EXAMPLES):
        raw.append(
            lax.dot_general(
                matrix,
                total[example],
                (((1,), (1,)), ((), ())),
                preferred_element_type=jnp.float32,
                precision=lax.Precision.HIGHEST,
            )
        )
    own_power = [jnp.sum(one * one, keepdims=True) for one in raw]
    row_of = lax.broadcasted_iota(jnp.int32, (8, 128), 0)
    tile = jnp.zeros((8, 128), jnp.float32)
    for example in range(EXAMPLES):
        tile = jnp.where(row_of == example, own_power[example], tile)
    powers[me] = tile

    def power_move(other):
        return pltpu.make_async_remote_copy(
            src_ref=powers.at[me],
            dst_ref=powers.at[me],
            send_sem=power_send.at[other],
            recv_sem=power_arrive.at[me],
            device_id={"expert": other},
            device_id_type=MESH,
        )

    for i in range(1, devices):
        power_move(lax.rem(me + i, devices)).start()

    @pl.loop(0, last)
    def _(distance):
        for step in range(steps):
            wait_sent(distance, step, (SIBLING,))

    for i in range(1, devices):
        other = lax.rem(me + i, devices)
        power_move(other).wait_send()
        pltpu.make_async_copy(powers.at[other], powers.at[other], power_arrive.at[other]).wait()

    power = jnp.sum(powers[...], axis=0)
    factor = lax.rsqrt(power / (devices * side * side) + 1e-06)
    for example in range(EXAMPLES):
        result_ref[example] = raw[example] * factor[example : example + 1, :1]


def on_device(devices, lines, acts, out_grad, routes, route_weight, w_gate, w_up, proj_in, proj_out):
    rows, depth = acts.shape
    top = routes.shape[1]
    width = w_gate.shape[2]
    side = proj_out.shape[1]
    pieces = len(row_chunks(rows, lines)[0]) + 1
    dma = pltpu.SemaphoreType.DMA
    scaled = pl.pallas_call(
        functools.partial(kernel, devices, lines),
        out_shape=jax.ShapeDtypeStruct((EXAMPLES, side, side), jnp.float32),
        in_specs=[pl.BlockSpec(memory_space=pl.ANY)] * 8,
        out_specs=pl.BlockSpec(memory_space=pltpu.VMEM),
        scratch_shapes=[
            pltpu.VMEM((devices, rows, depth), jnp.bfloat16),
            pltpu.VMEM((rows, depth), jnp.bfloat16),
            pltpu.VMEM((top, rows), jnp.int32),
            pltpu.VMEM((top, rows), jnp.float32),
            pltpu.VMEM((depth, width), jnp.bfloat16),
            pltpu.VMEM((depth, width), jnp.bfloat16),
            pltpu.VMEM((side, width), jnp.bfloat16),
            pltpu.VMEM((side, depth), jnp.bfloat16),
            pltpu.VMEM((devices, side + devices, rows), jnp.float32),
            pltpu.VMEM((EXAMPLES, side, width), jnp.float32),
            pltpu.VMEM((devices, 8, 128), jnp.float32),
            dma((8,)),
            dma((devices, pieces)),
            dma((4, devices, pieces)),
            dma((devices,)),
            dma((devices,)),
        ],
        compiler_params=pltpu.CompilerParams(
            collective_id=0, has_side_effects=True, vmem_limit_bytes=60 * 1024 * 1024
        ),
        cost_estimate=pl.CostEstimate(
            flops=2 * devices * rows * depth * 2 * width,
            bytes_accessed=2 * depth * width * 2,
            transcendentals=devices * rows * width,
        ),
    )(
        acts, out_grad, routes.T, route_weight.T, w_gate, w_up, proj_in.swapaxes(1, 2), proj_out.T
    )
    return scaled.reshape(1, EXAMPLES, side * side)


def solution(mesh):
    devices = mesh.shape["expert"]
    lines = 2 if devices == 16 else 1
    return jax.shard_map(
        functools.partial(on_device, devices, lines),
        mesh=mesh,
        in_specs=(
            P(("groups", "expert"), None),
            P(("groups", "expert"), None),
            P(("groups", "expert"), None),
            P(("groups", "expert"), None),
            P("expert", None, None),
            P("expert", None, None),
            P("expert", None, None),
            P(),
        ),
        out_specs=P("expert", "groups", None),
        check_vma=False,
    )
```

```python
import functools

import jax
import jax.numpy as jnp
from jax import lax
from jax.experimental import pallas as pl
from jax.experimental.pallas import tpu as pltpu
from jax.sharding import PartitionSpec as P

EXAMPLES = 2
MESH = pl.DeviceIdType.MESH
RIGHT, LEFT, ACROSS, SIBLING = 0, 1, 2, 3


def row_chunks(rows, lines):
    half, part = rows // 2, rows // 8
    if lines == 1:
        return ((0, half), (half, rows - half)), 2
    return ((0, 6 * part), (6 * part, part), (rows - part, part)), 2


def kernel(
    devices, lines, acts_ref, grad_ref, routes_ref, weight_ref, gate_ref, up_ref, in_ref, out_ref,
    result_ref,
    acts, grad, routes, weight, gate, up, proj_in, proj_out,
    notes, total, powers,
    local_sem, arrive_sem, send_sem, power_arrive, power_send,
):
    length = devices // 2 // lines
    chips = devices // 2
    rows = acts.shape[1]
    side = proj_out.shape[0]
    width = gate.shape[1]
    chunks, first_count = row_chunks(rows, lines)
    me = lax.axis_index("expert")
    core = lax.rem(me, 2)
    chip = me // 2
    line = lax.rem(chip, lines)
    place = chip // lines

    def block(at_place, at_line, at_core):
        return (jnp.clip(at_place, 0, length - 1) * lines + at_line) * 2 + at_core

    def sibling_of(index):
        return index + 1 - 2 * lax.rem(index, 2)

    loads = [
        pltpu.make_async_copy(grad_ref, grad, local_sem.at[0]),
        pltpu.make_async_copy(out_ref, proj_out, local_sem.at[1]),
        pltpu.make_async_copy(routes_ref, routes, local_sem.at[2]),
        pltpu.make_async_copy(weight_ref, weight, local_sem.at[3]),
        pltpu.make_async_copy(acts_ref, acts.at[me], local_sem.at[4]),
        pltpu.make_async_copy(gate_ref.at[0], gate, local_sem.at[5]),
        pltpu.make_async_copy(up_ref.at[0], up, local_sem.at[6]),
        pltpu.make_async_copy(in_ref.at[0], proj_in, local_sem.at[7]),
    ]
    for load in loads:
        load.start()

    targets = (
        block(place + 1, line, core),
        block(place - 1, line, core),
        block(place, lines - 1 - line, core),
        sibling_of(me),
    )
    has_right = place < length - 1
    has_left = place > 0
    other_line = lines - 1 - line

    neighbours = [(has_right, RIGHT), (has_left, LEFT), (True, SIBLING)]
    if lines > 1:
        neighbours.append((True, ACROSS))
    barrier = pltpu.get_barrier_semaphore()
    for present, way in neighbours:
        @pl.when(present)
        def _(way=way):
            pl.semaphore_signal(
                barrier, inc=1, device_id={"expert": targets[way]}, device_id_type=MESH
            )

    others = 1 + (lines - 1) + has_right.astype(jnp.int32) + has_left.astype(jnp.int32)
    pl.semaphore_wait(barrier, others)

    notes_chunk = len(chunks)

    def transfer(index, chunk, way, own=False):
        if chunk == notes_chunk:
            source = target = notes.at[index]
        else:
            start, count = chunks[chunk]
            source = target = acts.at[index, pl.ds(start, count)]
            if own:
                source = acts_ref.at[pl.ds(start, count)]
        return pltpu.make_async_remote_copy(
            src_ref=source,
            dst_ref=target,
            send_sem=send_sem.at[way, index, chunk],
            recv_sem=arrive_sem.at[index, chunk],
            device_id={"expert": targets[way]},
            device_id_type=MESH,
        )

    def own_notes():
        return [(present, me, notes_chunk, way) for present, way in neighbours]

    def own_moves():
        moves = []
        for chunk in range(first_count, len(chunks)):
            moves.append((True, me, chunk, ACROSS))
        for chunk in range(len(chunks)):
            moves.append((has_right, me, chunk, RIGHT))
            moves.append((has_left, me, chunk, LEFT))
            if chunk < first_count and lines > 1:
                moves.append((True, me, chunk, ACROSS))
            moves.append((True, me, chunk, SIBLING))
        return moves

    def arrivals(distance):
        listed = []
        for chunk in range(first_count, len(chunks)):
            present = distance == 1
            index = block(place, other_line, core)
            moves = [
                (present & has_right, index, chunk, RIGHT),
                (present & has_left, index, chunk, LEFT),
                (present, index, chunk, SIBLING),
            ]
            listed.append((present, index, chunk, moves))
        for chunk in (*range(first_count), notes_chunk, *range(first_count, len(chunks))):
            late = first_count <= chunk < notes_chunk
            for way in (RIGHT, LEFT):
                at = place - distance if way == RIGHT else place + distance
                inside = (at >= 0) if way == RIGHT else (at < length)
                onward = has_right if way == RIGHT else has_left
                present = (distance >= 1) & inside & (distance < length)
                index = block(at, line, core)
                moves = [(present & onward, index, chunk, way)]
                if lines > 1 and not late:
                    moves.append((present, index, chunk, ACROSS))
                moves.append((present, index, chunk, SIBLING))
                listed.append((present, index, chunk, moves))
                if lines == 1:
                    continue
                if late:
                    index = block(at, other_line, core)
                    moves = [(present & onward, index, chunk, way), (present, index, chunk, SIBLING)]
                    listed.append((present, index, chunk, moves))
                back = distance - 1
                at = place - back if way == RIGHT else place + back
                inside = (at >= 0) if way == RIGHT else (at < length)
                index = block(at, other_line, core)
                if not late:
                    present = (distance >= 1) & inside
                    if way == LEFT:
                        present = present & (back >= 1)
                    listed.append((present, index, chunk, [(present, index, chunk, SIBLING)]))
        return listed

    for present, index, chunk, way in own_moves():
        @pl.when(present)
        def _(index=index, chunk=chunk, way=way):
            transfer(index, chunk, way, own=True).start()

    for load in loads[:4]:
        load.wait()
    projected = lax.dot_general(
        proj_out[...], grad[...], (((1,), (1,)), ((), ())), preferred_element_type=jnp.float32
    )
    names = routes[...]
    scales = weight[...]

    notes[me, :side] = projected
    for expert in range(devices):
        hit = names == expert
        notes[me, side + expert : side + expert + 1] = jnp.sum(
            jnp.where(hit, scales, 0.0), axis=0, keepdims=True
        )
    for present, index, chunk, way in own_notes():
        @pl.when(present)
        def _(index=index, chunk=chunk, way=way):
            transfer(index, chunk, way).start()

    total[...] = jnp.zeros_like(total)
    for load in loads[4:]:
        load.wait()

    def compute(chip_index):
        x = acts[pl.ds(2 * chip_index, 2)].reshape(2 * rows, acts.shape[2])
        pair = [
            notes[2 * chip_index + part, :side] * notes[2 * chip_index + part, pl.ds(side + me, 1)]
            for part in range(2)
        ]
        pair = jnp.concatenate(pair, axis=1).astype(jnp.bfloat16)
        example = chip_index // (chips // EXAMPLES)
        step = 256
        for start in range(0, width, step):
            gated = jnp.dot(x, gate[:, start : start + step], preferred_element_type=jnp.float32)
            upper = jnp.dot(x, up[:, start : start + step], preferred_element_type=jnp.float32)
            hidden = (gated / (1.0 + jnp.exp(-gated)) * upper).astype(jnp.bfloat16)
            total[example, :, start : start + step] += jnp.dot(
                pair, hidden, preferred_element_type=jnp.float32
            )

    @pl.loop(0, length + (1 if lines > 1 else 0))
    def _(distance):
        for present, index, chunk, moves in arrivals(distance):
            @pl.when(present)
            def _(index=index, chunk=chunk):
                transfer(index, chunk, SIBLING).wait_recv()

            for wanted, index, chunk, way in moves:
                @pl.when(wanted)
                def _(index=index, chunk=chunk, way=way):
                    transfer(index, chunk, way).start()

        @pl.loop(0, 4 if lines > 1 else 2)
        def _(unit):
            partner = unit // 2
            leftward = lax.rem(unit, 2)
            far = distance - partner
            at = place - far + 2 * far * leftward
            present = (far >= leftward) & (at >= 0) & (at < length)
            index = block(at, line + partner * (other_line - line), core)

            @pl.when(present)
            def _():
                for chunk in range(len(chunks) + 1):
                    transfer(sibling_of(index), chunk, SIBLING).wait_recv()

                compute(index // 2)

    raw = []
    matrix = proj_in[...].astype(jnp.float32)
    for example in range(EXAMPLES):
        raw.append(
            lax.dot_general(
                matrix,
                total[example],
                (((1,), (1,)), ((), ())),
                preferred_element_type=jnp.float32,
                precision=lax.Precision.HIGHEST,
            )
        )
    own_power = [jnp.sum(one * one, keepdims=True) for one in raw]
    row_of = lax.broadcasted_iota(jnp.int32, (8, 128), 0)
    tile = jnp.zeros((8, 128), jnp.float32)
    for example in range(EXAMPLES):
        tile = jnp.where(row_of == example, own_power[example], tile)
    powers[me] = tile

    def power_move(other):
        return pltpu.make_async_remote_copy(
            src_ref=powers.at[me],
            dst_ref=powers.at[me],
            send_sem=power_send.at[other],
            recv_sem=power_arrive.at[me],
            device_id={"expert": other},
            device_id_type=MESH,
        )

    for i in range(1, devices):
        power_move(lax.rem(me + i, devices)).start()

    for present, index, chunk, way in own_moves() + own_notes():
        @pl.when(present)
        def _(index=index, chunk=chunk, way=way):
            transfer(index, chunk, way, own=True).wait_send()

    @pl.loop(0, length + (1 if lines > 1 else 0))
    def _(distance):
        for _, _, _, moves in arrivals(distance):
            for wanted, index, chunk, way in moves:
                @pl.when(wanted)
                def _(index=index, chunk=chunk, way=way):
                    transfer(index, chunk, way).wait_send()

    for i in range(1, devices):
        other = lax.rem(me + i, devices)
        power_move(other).wait_send()
        pltpu.make_async_copy(powers.at[other], powers.at[other], power_arrive.at[other]).wait()

    power = jnp.sum(powers[...], axis=0)
    factor = lax.rsqrt(power / (devices * side * side) + 1e-06)
    for example in range(EXAMPLES):
        result_ref[example] = raw[example] * factor[example : example + 1, :1]


def on_device(devices, lines, acts, out_grad, routes, route_weight, w_gate, w_up, proj_in, proj_out):
    rows, depth = acts.shape
    top = routes.shape[1]
    width = w_gate.shape[2]
    side = proj_out.shape[1]
    pieces = len(row_chunks(rows, lines)[0]) + 1
    dma = pltpu.SemaphoreType.DMA
    scaled = pl.pallas_call(
        functools.partial(kernel, devices, lines),
        out_shape=jax.ShapeDtypeStruct((EXAMPLES, side, side), jnp.float32),
        in_specs=[pl.BlockSpec(memory_space=pl.ANY)] * 8,
        out_specs=pl.BlockSpec(memory_space=pltpu.VMEM),
        scratch_shapes=[
            pltpu.VMEM((devices, rows, depth), jnp.bfloat16),
            pltpu.VMEM((rows, depth), jnp.bfloat16),
            pltpu.VMEM((top, rows), jnp.int32),
            pltpu.VMEM((top, rows), jnp.float32),
            pltpu.VMEM((depth, width), jnp.bfloat16),
            pltpu.VMEM((depth, width), jnp.bfloat16),
            pltpu.VMEM((side, width), jnp.bfloat16),
            pltpu.VMEM((side, depth), jnp.bfloat16),
            pltpu.VMEM((devices, side + devices, rows), jnp.float32),
            pltpu.VMEM((EXAMPLES, side, width), jnp.float32),
            pltpu.VMEM((devices, 8, 128), jnp.float32),
            dma((8,)),
            dma((devices, pieces)),
            dma((4, devices, pieces)),
            dma((devices,)),
            dma((devices,)),
        ],
        compiler_params=pltpu.CompilerParams(
            collective_id=0, has_side_effects=True, vmem_limit_bytes=60 * 1024 * 1024
        ),
        cost_estimate=pl.CostEstimate(
            flops=2 * devices * rows * depth * 2 * width,
            bytes_accessed=2 * depth * width * 2,
            transcendentals=devices * rows * width,
        ),
    )(
        acts, out_grad, routes.T, route_weight.T, w_gate, w_up, proj_in.swapaxes(1, 2), proj_out.T
    )
    return scaled.reshape(1, EXAMPLES, side * side)


def solution(mesh):
    devices = mesh.shape["expert"]
    lines = 2 if devices == 16 else 1
    return jax.shard_map(
        functools.partial(on_device, devices, lines),
        mesh=mesh,
        in_specs=(
            P(("groups", "expert"), None),
            P(("groups", "expert"), None),
            P(("groups", "expert"), None),
            P(("groups", "expert"), None),
            P("expert", None, None),
            P("expert", None, None),
            P("expert", None, None),
            P(),
        ),
        out_specs=P("expert", "groups", None),
        check_vma=False,
    )
```

```python
import functools

import jax
import jax.numpy as jnp
from jax import lax
from jax.experimental import pallas as pl
from jax.experimental.pallas import tpu as pltpu
from jax.sharding import PartitionSpec as P

EXAMPLES = 2
MESH = pl.DeviceIdType.MESH
RIGHT, LEFT, ACROSS, SIBLING = 0, 1, 2, 3


def row_chunks(rows, lines):
    half, part = rows // 2, rows // 8
    if lines == 1:
        return ((0, half), (half, rows - half)), 2
    return ((0, half), (half, 3 * part), (rows - part, part)), 2


def kernel(
    devices, lines, acts_ref, grad_ref, routes_ref, weight_ref, gate_ref, up_ref, in_ref, out_ref,
    result_ref,
    acts, grad, routes, weight, gate, up, proj_in, proj_out,
    notes, total, powers,
    local_sem, arrive_sem, send_sem, power_arrive, power_send,
):
    length = devices // 2 // lines
    chips = devices // 2
    rows = acts.shape[1]
    side = proj_out.shape[0]
    width = gate.shape[1]
    chunks, first_count = row_chunks(rows, lines)
    me = lax.axis_index("expert")
    core = lax.rem(me, 2)
    chip = me // 2
    line = lax.rem(chip, lines)
    place = chip // lines

    def block(at_place, at_line, at_core):
        return (jnp.clip(at_place, 0, length - 1) * lines + at_line) * 2 + at_core

    def sibling_of(index):
        return index + 1 - 2 * lax.rem(index, 2)

    loads = [
        pltpu.make_async_copy(grad_ref, grad, local_sem.at[0]),
        pltpu.make_async_copy(out_ref, proj_out, local_sem.at[1]),
        pltpu.make_async_copy(routes_ref, routes, local_sem.at[2]),
        pltpu.make_async_copy(weight_ref, weight, local_sem.at[3]),
        pltpu.make_async_copy(acts_ref, acts.at[me], local_sem.at[4]),
        pltpu.make_async_copy(gate_ref.at[0], gate, local_sem.at[5]),
        pltpu.make_async_copy(up_ref.at[0], up, local_sem.at[6]),
        pltpu.make_async_copy(in_ref.at[0], proj_in, local_sem.at[7]),
    ]
    for load in loads:
        load.start()

    targets = (
        block(place + 1, line, core),
        block(place - 1, line, core),
        block(place, lines - 1 - line, core),
        sibling_of(me),
    )
    has_right = place < length - 1
    has_left = place > 0
    other_line = lines - 1 - line

    neighbours = [(has_right, RIGHT), (has_left, LEFT), (True, SIBLING)]
    if lines > 1:
        neighbours.append((True, ACROSS))
    barrier = pltpu.get_barrier_semaphore()
    for present, way in neighbours:
        @pl.when(present)
        def _(way=way):
            pl.semaphore_signal(
                barrier, inc=1, device_id={"expert": targets[way]}, device_id_type=MESH
            )

    others = 1 + (lines - 1) + has_right.astype(jnp.int32) + has_left.astype(jnp.int32)
    pl.semaphore_wait(barrier, others)

    notes_chunk = len(chunks)

    def transfer(index, chunk, way, own=False):
        if chunk == notes_chunk:
            source = target = notes.at[index]
        else:
            start, count = chunks[chunk]
            source = target = acts.at[index, pl.ds(start, count)]
            if own:
                source = acts_ref.at[pl.ds(start, count)]
        return pltpu.make_async_remote_copy(
            src_ref=source,
            dst_ref=target,
            send_sem=send_sem.at[way, index, chunk],
            recv_sem=arrive_sem.at[index, chunk],
            device_id={"expert": targets[way]},
            device_id_type=MESH,
        )

    def own_notes():
        return [(present, me, notes_chunk, way) for present, way in neighbours]

    def own_moves():
        moves = []
        for chunk in range(first_count, len(chunks)):
            moves.append((True, me, chunk, ACROSS))
        for chunk in range(len(chunks)):
            moves.append((has_right, me, chunk, RIGHT))
            moves.append((has_left, me, chunk, LEFT))
            if chunk < first_count and lines > 1:
                moves.append((True, me, chunk, ACROSS))
            moves.append((True, me, chunk, SIBLING))
        return moves

    def arrivals(distance):
        listed = []
        for chunk in range(first_count, len(chunks)):
            present = distance == 1
            index = block(place, other_line, core)
            moves = [
                (present & has_right, index, chunk, RIGHT),
                (present & has_left, index, chunk, LEFT),
                (present, index, chunk, SIBLING),
            ]
            listed.append((present, index, chunk, moves))
        for chunk in (*range(first_count), notes_chunk, *range(first_count, len(chunks))):
            late = first_count <= chunk < notes_chunk
            for way in (RIGHT, LEFT):
                at = place - distance if way == RIGHT else place + distance
                inside = (at >= 0) if way == RIGHT else (at < length)
                onward = has_right if way == RIGHT else has_left
                present = (distance >= 1) & inside & (distance < length)
                index = block(at, line, core)
                moves = [(present & onward, index, chunk, way)]
                if lines > 1 and not late:
                    moves.append((present, index, chunk, ACROSS))
                moves.append((present, index, chunk, SIBLING))
                listed.append((present, index, chunk, moves))
                if lines == 1:
                    continue
                if late:
                    index = block(at, other_line, core)
                    moves = [(present & onward, index, chunk, way), (present, index, chunk, SIBLING)]
                    listed.append((present, index, chunk, moves))
                back = distance - 1
                at = place - back if way == RIGHT else place + back
                inside = (at >= 0) if way == RIGHT else (at < length)
                index = block(at, other_line, core)
                if not late:
                    present = (distance >= 1) & inside
                    if way == LEFT:
                        present = present & (back >= 1)
                    listed.append((present, index, chunk, [(present, index, chunk, SIBLING)]))
        return listed

    def start_own(later):
        for present, index, chunk, way in own_moves():
            if later == (chunk > 0 and (way != ACROSS or chunk < first_count)):
                @pl.when(present)
                def _(index=index, chunk=chunk, way=way):
                    transfer(index, chunk, way, own=True).start()

    start_own(False)

    for load in loads[:4]:
        load.wait()
    projected = lax.dot_general(
        proj_out[...], grad[...], (((1,), (1,)), ((), ())), preferred_element_type=jnp.float32
    )
    names = routes[...]
    scales = weight[...]

    start_own(True)
    notes[me, :side] = projected
    for expert in range(devices):
        hit = names == expert
        notes[me, side + expert : side + expert + 1] = jnp.sum(
            jnp.where(hit, scales, 0.0), axis=0, keepdims=True
        )
    for present, index, chunk, way in own_notes():
        @pl.when(present)
        def _(index=index, chunk=chunk, way=way):
            transfer(index, chunk, way).start()

    total[...] = jnp.zeros_like(total)
    for load in loads[4:]:
        load.wait()

    def compute(chip_index):
        x = acts[pl.ds(2 * chip_index, 2)].reshape(2 * rows, acts.shape[2])
        pair = [
            notes[2 * chip_index + part, :side] * notes[2 * chip_index + part, pl.ds(side + me, 1)]
            for part in range(2)
        ]
        pair = jnp.concatenate(pair, axis=1).astype(jnp.bfloat16)
        example = chip_index // (chips // EXAMPLES)
        step = 256
        for start in range(0, width, step):
            gated = jnp.dot(x, gate[:, start : start + step], preferred_element_type=jnp.float32)
            upper = jnp.dot(x, up[:, start : start + step], preferred_element_type=jnp.float32)
            hidden = (gated / (1.0 + jnp.exp(-gated)) * upper).astype(jnp.bfloat16)
            total[example, :, start : start + step] += jnp.dot(
                pair, hidden, preferred_element_type=jnp.float32
            )

    @pl.loop(0, length + (1 if lines > 1 else 0))
    def _(distance):
        for present, index, chunk, moves in arrivals(distance):
            @pl.when(present)
            def _(index=index, chunk=chunk):
                transfer(index, chunk, SIBLING).wait_recv()

            for wanted, index, chunk, way in moves:
                @pl.when(wanted)
                def _(index=index, chunk=chunk, way=way):
                    transfer(index, chunk, way).start()

        @pl.loop(0, 4 if lines > 1 else 2)
        def _(unit):
            partner = unit // 2
            leftward = lax.rem(unit, 2)
            far = distance - partner
            at = place - far + 2 * far * leftward
            present = (far >= leftward) & (at >= 0) & (at < length)
            index = block(at, line + partner * (other_line - line), core)

            @pl.when(present)
            def _():
                for chunk in range(len(chunks) + 1):
                    transfer(sibling_of(index), chunk, SIBLING).wait_recv()

                compute(index // 2)

    raw = []
    matrix = proj_in[...].astype(jnp.float32)
    for example in range(EXAMPLES):
        raw.append(
            lax.dot_general(
                matrix,
                total[example],
                (((1,), (1,)), ((), ())),
                preferred_element_type=jnp.float32,
                precision=lax.Precision.HIGHEST,
            )
        )
    own_power = [jnp.sum(one * one, keepdims=True) for one in raw]
    row_of = lax.broadcasted_iota(jnp.int32, (8, 128), 0)
    tile = jnp.zeros((8, 128), jnp.float32)
    for example in range(EXAMPLES):
        tile = jnp.where(row_of == example, own_power[example], tile)
    powers[me] = tile

    def power_move(other):
        return pltpu.make_async_remote_copy(
            src_ref=powers.at[me],
            dst_ref=powers.at[me],
            send_sem=power_send.at[other],
            recv_sem=power_arrive.at[me],
            device_id={"expert": other},
            device_id_type=MESH,
        )

    for i in range(1, devices):
        power_move(lax.rem(me + i, devices)).start()

    for present, index, chunk, way in own_moves() + own_notes():
        @pl.when(present)
        def _(index=index, chunk=chunk, way=way):
            transfer(index, chunk, way, own=True).wait_send()

    @pl.loop(0, length + (1 if lines > 1 else 0))
    def _(distance):
        for _, _, _, moves in arrivals(distance):
            for wanted, index, chunk, way in moves:
                @pl.when(wanted)
                def _(index=index, chunk=chunk, way=way):
                    transfer(index, chunk, way).wait_send()

    for i in range(1, devices):
        other = lax.rem(me + i, devices)
        power_move(other).wait_send()
        pltpu.make_async_copy(powers.at[other], powers.at[other], power_arrive.at[other]).wait()

    power = jnp.sum(powers[...], axis=0)
    factor = lax.rsqrt(power / (devices * side * side) + 1e-06)
    for example in range(EXAMPLES):
        scaled = raw[example] * factor[example : example + 1, :1]
        for row in range(side):
            result_ref[0, example : example + 1, row * side : (row + 1) * side] = scaled[row : row + 1]


def on_device(devices, lines, acts, out_grad, routes, route_weight, w_gate, w_up, proj_in, proj_out):
    rows, depth = acts.shape
    top = routes.shape[1]
    width = w_gate.shape[2]
    side = proj_out.shape[1]
    pieces = len(row_chunks(rows, lines)[0]) + 1
    dma = pltpu.SemaphoreType.DMA
    scaled = pl.pallas_call(
        functools.partial(kernel, devices, lines),
        out_shape=jax.ShapeDtypeStruct((1, EXAMPLES, side * side), jnp.float32),
        in_specs=[pl.BlockSpec(memory_space=pl.ANY)] * 8,
        out_specs=pl.BlockSpec(memory_space=pltpu.VMEM),
        scratch_shapes=[
            pltpu.VMEM((devices, rows, depth), jnp.bfloat16),
            pltpu.VMEM((rows, depth), jnp.bfloat16),
            pltpu.VMEM((top, rows), jnp.int32),
            pltpu.VMEM((top, rows), jnp.float32),
            pltpu.VMEM((depth, width), jnp.bfloat16),
            pltpu.VMEM((depth, width), jnp.bfloat16),
            pltpu.VMEM((side, width), jnp.bfloat16),
            pltpu.VMEM((side, depth), jnp.bfloat16),
            pltpu.VMEM((devices, side + devices, rows), jnp.float32),
            pltpu.VMEM((EXAMPLES, side, width), jnp.float32),
            pltpu.VMEM((devices, 8, 128), jnp.float32),
            dma((8,)),
            dma((devices, pieces)),
            dma((4, devices, pieces)),
            dma((devices,)),
            dma((devices,)),
        ],
        compiler_params=pltpu.CompilerParams(
            collective_id=0, has_side_effects=True, vmem_limit_bytes=60 * 1024 * 1024
        ),
        cost_estimate=pl.CostEstimate(
            flops=2 * devices * rows * depth * 2 * width,
            bytes_accessed=2 * depth * width * 2,
            transcendentals=devices * rows * width,
        ),
    )(
        acts, out_grad, routes.T, route_weight.T, w_gate, w_up, proj_in.swapaxes(1, 2), proj_out.T
    )
    return scaled


def solution(mesh):
    devices = mesh.shape["expert"]
    lines = 2 if devices == 16 else 1
    return jax.shard_map(
        functools.partial(on_device, devices, lines),
        mesh=mesh,
        in_specs=(
            P(("groups", "expert"), None),
            P(("groups", "expert"), None),
            P(("groups", "expert"), None),
            P(("groups", "expert"), None),
            P("expert", None, None),
            P("expert", None, None),
            P("expert", None, None),
            P(),
        ),
        out_specs=P("expert", "groups", None),
        check_vma=False,
    )
```
